128 devices in a mesh: rows: 32 (over x, z, y_hi), cols: 4 (over y_lo, core).
Axes of the slice: x: 4, y: 4 (y_hi: 2, y_lo: 2; y = y_hi * 2 + y_lo), z: 4, core: 2. Of those that a mesh axis runs over, the one named last changes fastest.
Arguments:
- snapshots: float32 [64, 2, 512, 512], P('cols', None, 'rows'), may hold values from -6 to 6
- adjoint: bfloat16 [2048, 2, 512, 512], P('cols', None, 'rows'), may hold values from -0.0078125 to 0.0078125
- base_flow: float32 [512], replicated, may hold values from 0.3 to 1
- shear: float32 [512], replicated, may hold values from -1 to 1
Outputs:
- advanced: float32 [64, 2, 512, 512], P('cols', None, 'rows')
- gram: float32 [2, 64, 2048], P(None, None, 'cols')
The draws below stay inside these ranges and needn't reach their ends.
All inputs are finite; a program needn't handle non-finite values.
Results may differ from the reference program's by a relative error of at most 0.0031.
Values may be sent and summed in bfloat16 or wider, within the bound.
A program may use at most 128 MiB of HBM per device.

```python
import math
import jax
import jax.numpy as jnp

NY = 512
NX = 512
SNAPS = 64
ADJS = 2048


def levels(stream_key, dims, pieces, low, top_value):
    factor_of, own = 1.0, jax.random.fold_in(stream_key, 6)
    for axis_at, shards_of in pieces:
        steps = jnp.exp(jax.random.uniform(jax.random.fold_in(own, axis_at), (shards_of,), jnp.float32, low / len(pieces), top_value / len(pieces)))
        factor_of = factor_of * jnp.repeat(steps, dims[axis_at] // shards_of).reshape([-1 if axis == axis_at else 1 for axis in range(len(dims))])
    return factor_of


def scatter_about(rng, dims, spread, reach, split=(), dtype=jnp.bfloat16):
    entries = jax.random.normal(rng, dims, jnp.float32) * spread
    if len(split) > 0:
        entries = levels(rng, dims, split, -0.22, 0.18) * entries
    return jnp.clip(entries, min=-reach, max=reach).astype(dtype)


def setup_inputs(seed: int = 0) -> dict:
    splits = jax.random.split(jax.random.key(seed), 5)
    return {
        "snapshots": scatter_about(splits[0], (SNAPS, 2, NX, NY), 1.0, 6.0, ((0, 4), (2, 32)), jnp.float32),
        "adjoint": scatter_about(splits[1], (ADJS, 2, NX, NY), (2 * NX * NY) ** -0.5, 0.0078125, ((0, 4), (2, 32))),
        "base_flow": jnp.clip(jnp.exp(jax.random.uniform(splits[2], (NY,), jnp.float32, math.log(0.3), math.log(1.0))), 0.3, 1.0),
        "shear": jnp.clip(jax.random.uniform(splits[3], (NY,), jnp.float32, -1.0, 1.0), -1.0, 1.0),
    }


def advance(field, base_flow, shear):
    ahead = jnp.roll(field, -1, axis=2)
    behind = jnp.roll(field, 1, axis=2)
    padded = jnp.pad(field, ((0, 0), (0, 0), (0, 0), (1, 1)))
    laplace = ahead + behind + padded[..., 2:] + padded[..., :-2] - 4.0 * field
    result = field + 0.1 * laplace - 0.3 * base_flow * (ahead - behind)
    coupling = 0.3 * shear * field[:, 1]
    return result.at[:, 0].add(-coupling)


def reference(snapshots, adjoint, base_flow, shear):
    state_one = advance(snapshots, base_flow, shear)
    advanced = advance(state_one, base_flow, shear)
    adjoint_flat = adjoint.reshape(adjoint.shape[0], -1)
    first = jnp.dot(state_one.astype(jnp.bfloat16).reshape(state_one.shape[0], -1), adjoint_flat.T, preferred_element_type=jnp.float32)
    second = jnp.dot(advanced.astype(jnp.bfloat16).reshape(advanced.shape[0], -1), adjoint_flat.T, preferred_element_type=jnp.float32)
    return advanced, jnp.stack([first, second])
```

```python
import functools

import jax
import jax.numpy as jnp
from jax import lax
from jax.experimental import pallas as pl
from jax.experimental.pallas import tpu as pltpu
from jax.sharding import PartitionSpec as P

ROWS = 32
SNAPS = 16
ADJS = 512
NX = 16
NY = 512
BLOCK = 32
LOADS = ADJS // BLOCK
RING = 8
SCALE = 8192.0
TINY = 1e-37
CUTS = ((2, 6), (8, 4), (12, 4), (16, 2))
MESH = pl.DeviceIdType.MESH
NT = (((1,), (1,)), ((), ()))
F32 = jnp.float32
LOW = jnp.bfloat16


def encode(value):
    scaled = value * SCALE
    square = scaled * scaled
    return ((scaled * jnp.abs(scaled)) * (square * (square * square))).astype(LOW)


def decode(code):
    wide = code.astype(F32)
    half = lax.rsqrt(jnp.maximum(jnp.abs(wide), TINY))
    eighth = lax.rsqrt(lax.rsqrt(half))
    return (wide * half) * (eighth * eighth * eighth) * (1.0 / SCALE)


def kernel(
    snaps_hbm, adj_hbm, base_ref, shear_ref,
    adv_hbm, gram_ref,
    snaps, coef, own, own_one, own_adv, adv_out, code, far_code, far, far_one,
    low, adj_raw, adj, total, part, gather, result,
    io_sem, load_sem, halo_send, halo_recv, far_send, far_recv,
    pass_send, pass_recv, side_send, side_recv, sum_sem,
):
    row = lax.axis_index("rows")
    col = lax.axis_index("cols")
    core = col % 2
    side = col + 1 - 2 * core
    far_col = (col + 2) % 4
    up = (row + 1) % ROWS
    down = (row + ROWS - 1) % ROWS

    def load(i):
        return pltpu.make_async_copy(
            adj_hbm.at[pl.ds(pl.multiple_of(i * BLOCK, BLOCK), BLOCK)],
            adj_raw.at[i % RING],
            load_sem.at[i % RING],
        )

    snaps_in = pltpu.make_async_copy(snaps_hbm, snaps, io_sem.at[0])
    snaps_in.start()
    for i in range(RING):
        load(i).start()

    barrier = pltpu.get_barrier_semaphore()
    pl.semaphore_signal(barrier, inc=1, device_id=(row, far_col), device_id_type=MESH)
    pl.semaphore_signal(barrier, inc=1, device_id=(row, side), device_id_type=MESH)
    pl.semaphore_signal(barrier, inc=1, device_id=(up, far_col), device_id_type=MESH)
    pl.semaphore_signal(barrier, inc=1, device_id=(down, far_col), device_id_type=MESH)

    def greet(d, _):
        pl.semaphore_signal(
            barrier, inc=1, device_id=((row + d) % ROWS, col), device_id_type=MESH
        )
        return 0

    lax.fori_loop(1, ROWS, greet, 0)

    lane = lax.broadcasted_iota(jnp.int32, (SNAPS, NY), 1)
    base = jnp.broadcast_to(base_ref[...], (SNAPS, NY))
    coef[0] = 0.1 - 0.3 * base
    coef[1] = 0.1 + 0.3 * base
    coef[2] = jnp.where(lane == NY - 1, 0.0, 0.1)
    coef[3] = jnp.where(lane == 0, 0.0, 0.1)
    coef[4] = 0.3 * jnp.broadcast_to(shear_ref[...], (SNAPS, NY))

    snaps_in.wait()
    for c in range(2):
        turned = jnp.swapaxes(snaps[:, c], 0, 1)
        own[pl.ds(2, NX), c] = turned
        code[:, c] = encode(turned)

    pl.semaphore_wait(barrier, ROWS - 1 + 4)

    halos = []
    for i, (to_row, to_col) in enumerate(
        ((up, col), (down, col), (up, far_col), (down, far_col))
    ):
        src = code.at[pl.ds(NX - 2, 2)] if i % 2 == 0 else code.at[pl.ds(0, 2)]
        at = 0 if i % 2 == 0 else NX + 2
        if i < 2:
            dst = own_halo(far_code, at)
        else:
            dst = far_code.at[pl.ds(at, 2), :, pl.ds(pl.multiple_of(core * SNAPS, SNAPS), SNAPS)]
        halos.append(
            pltpu.make_async_remote_copy(
                src, dst, halo_send.at[i], halo_recv.at[i],
                device_id=(to_row, to_col), device_id_type=MESH,
            )
        )
    fars = []
    for j, (at, count) in enumerate(CUTS):
        fars.append(
            pltpu.make_async_remote_copy(
                code.at[pl.ds(at - 2, count)],
                far_code.at[pl.ds(at, count), :, pl.ds(pl.multiple_of(core * SNAPS, SNAPS), SNAPS)],
                far_send.at[j], far_recv.at[j],
                device_id=(row, far_col), device_id_type=MESH,
            )
        )
    for copy in halos:
        copy.start()
    for copy in fars:
        copy.start()

    def passing(k, at, count):
        piece = far_code.at[pl.ds(at, count), :, pl.ds(pl.multiple_of(core * SNAPS, SNAPS), SNAPS)]
        return pltpu.make_async_remote_copy(
            piece, piece, pass_send.at[k], pass_recv.at[k],
            device_id=(row, side), device_id_type=MESH,
        )

    passes = [passing(j, at, count) for j, (at, count) in enumerate(CUTS)]
    passes += [passing(4, 0, 2), passing(5, NX + 2, 2)]

    def turn(i, _):
        load(i).wait()
        for c in range(2):
            block = jnp.swapaxes(adj_raw[i % RING, :, c], 0, 1)
            for x in range(NX):
                adj[2 * x + c, pl.ds(pl.multiple_of(i * BLOCK, BLOCK), BLOCK)] = block[x]

        @pl.when(i + RING < LOADS)
        def _():
            load(i + RING).start()

        return 0

    def step(read, x):
        result = []
        flow = [read(x, 0), read(x, 1)]
        for c in range(2):
            here = flow[c]
            value = 0.6 * here
            value += coef[0] * read(x + 1, c) + coef[1] * read(x - 1, c)
            value += coef[2] * pltpu.roll(here, NY - 1, 1) + coef[3] * pltpu.roll(here, 1, 1)
            if c == 0:
                value -= coef[4] * flow[1]
            result.append(value)
        return result

    lax.fori_loop(0, LOADS // 2, turn, 0)

    for i in range(2):
        halos[i].wait_recv()
        at = 0 if i == 0 else NX + 2
        for k in range(2):
            for c in range(2):
                own[at + k, c] = decode(own_halo(far_code, at)[k, c])

    own_at = pl.multiple_of(col * SNAPS, SNAPS)

    def own_first(x, _):
        values = step(lambda k, c: own[k + 1, c], x)
        for c in range(2):
            own_one[x, c] = values[c]
        return 0

    lax.fori_loop(0, NX + 2, own_first, 0)

    def own_second(x, _):
        values = step(lambda k, c: own_one[k + 1, c], x)
        for c in range(2):
            own_adv[x, c] = values[c]
            low[2 * x + c, pl.ds(own_at, SNAPS)] = own_one[x + 1, c].astype(LOW)
            low[2 * x + c, pl.ds(own_at + 64, SNAPS)] = values[c].astype(LOW)
        return 0

    lax.fori_loop(0, NX, own_second, 0)

    sides = []
    for k in range(2):
        piece = low.at[:, pl.ds(own_at + 64 * k, SNAPS)]
        sides.append(
            pltpu.make_async_remote_copy(
                piece, piece, side_send.at[k], side_recv.at[k],
                device_id=(row, side), device_id_type=MESH,
            )
        )
    for copy in sides:
        copy.start()

    for k in range(2):
        halos[2 + k].wait_recv()
        passes[4 + k].start()
    fars[0].wait_recv()
    passes[0].start()

    lax.fori_loop(LOADS // 2, LOADS, turn, 0)

    for c in range(2):
        adv_out[:, c] = jnp.swapaxes(own_adv[:, c], 0, 1)
    adv_copy = pltpu.make_async_copy(adv_out, adv_hbm, io_sem.at[1])
    adv_copy.start()

    far_at = pl.multiple_of(((col // 2 + 1) % 2) * 32, 32)

    def states(part_at, first, count, x_one, n_one, x_two):
        at = pl.multiple_of(part_at * SNAPS, SNAPS)

        def widen(k, _):
            for c in range(2):
                far[k, c, pl.ds(at, SNAPS)] = decode(far_code[k, c, pl.ds(at, SNAPS)])
            return 0

        lax.fori_loop(first, first + count, widen, 0)

        def one(x, _):
            values = step(lambda k, c: far[k + 1, c, pl.ds(at, SNAPS)], x)
            for c in range(2):
                far_one[x, c, pl.ds(at, SNAPS)] = values[c]
            return 0

        lax.fori_loop(x_one, x_one + n_one, one, 0)
        low_at = pl.multiple_of(far_at + at, SNAPS)

        def two(x, _):
            values = step(lambda k, c: far_one[k + 1, c, pl.ds(at, SNAPS)], x)
            for c in range(2):
                low[2 * x + c, pl.ds(low_at, SNAPS)] = far_one[x + 1, c, pl.ds(at, SNAPS)].astype(LOW)
                low[2 * x + c, pl.ds(low_at + 64, SNAPS)] = values[c].astype(LOW)
            return 0

        lax.fori_loop(x_two, x_two + 4, two, 0)

    def multiply(j):
        def body(k, _):
            at = 8 * j + 4 * k
            left = jnp.concatenate([low[at + i] for i in range(4)], axis=1)
            right = jnp.concatenate([adj[at + i] for i in range(4)], axis=1)
            total[...] += lax.dot_general(left, right, NT, preferred_element_type=F32)
            return 0

        lax.fori_loop(0, 2, body, 0)

    total[...] = jnp.zeros((128, ADJS), F32)
    for j in range(4):
        if j > 0:
            fars[j].wait_recv()
            passes[j].start()
        first, count = (0, 8) if j == 0 else (4 * j + 4, 4)
        x_one, n_one = (0, 6) if j == 0 else (4 * j + 2, 4)
        states(core, first, count, x_one, n_one, 4 * j)
        if j == 0:
            passes[4].wait_recv()
            passes[5].wait_recv()
            sides[0].wait_recv()
            sides[1].wait_recv()
        passes[j].wait_recv()
        states(1 - core, first, count, x_one, n_one, 4 * j)
        multiply(j)

    for t in range(ROWS):
        part[t] = total[pl.ds(16 * (t // 4), 16), pl.ds(128 * (t % 4), 128)]

    def scatter(d, _):
        to = (row + d) % ROWS
        pltpu.make_async_remote_copy(
            part.at[to], gather.at[row], sum_sem.at[0], sum_sem.at[1],
            device_id=(to, col), device_id_type=MESH,
        ).start()
        return 0

    lax.fori_loop(1, ROWS, scatter, 0)
    gather[row] = part[row]
    others = gather.at[pl.ds(0, ROWS - 1)]
    pltpu.make_async_copy(others, others, sum_sem.at[1]).wait()
    piece = gather[0]
    for t in range(1, ROWS):
        piece = piece + gather[t]
    result[row] = piece

    def spread(d, _):
        to = (row + d) % ROWS
        pltpu.make_async_remote_copy(
            result.at[row], result.at[row], sum_sem.at[2], sum_sem.at[3],
            device_id=(to, col), device_id_type=MESH,
        ).start()
        return 0

    lax.fori_loop(1, ROWS, spread, 0)
    adv_copy.wait()
    for copy in halos + fars + passes + sides:
        copy.wait_send()
    pltpu.make_async_copy(others, others, sum_sem.at[0]).wait()
    pltpu.make_async_copy(others, others, sum_sem.at[3]).wait()
    for t in range(ROWS):
        at = 16 * (t // 4)
        gram_ref[at // 64, pl.ds(at % 64, 16), pl.ds(128 * (t % 4), 128)] = result[t]
    pltpu.make_async_copy(others, others, sum_sem.at[2]).wait()


def own_halo(ref, at):
    return ref.at[pl.ds(NX + 4 + (0 if at == 0 else 2), 2), :, pl.ds(0, SNAPS)]


def per_device(snapshots, adjoint, base_flow, shear):
    vmem = pltpu.VMEM
    return pl.pallas_call(
        kernel,
        out_shape=(
            jax.ShapeDtypeStruct((SNAPS, 2, NX, NY), F32),
            jax.ShapeDtypeStruct((2, 64, ADJS), F32),
        ),
        in_specs=[
            pl.BlockSpec(memory_space=pl.ANY),
            pl.BlockSpec(memory_space=pl.ANY),
            pl.BlockSpec(memory_space=vmem),
            pl.BlockSpec(memory_space=vmem),
        ],
        out_specs=(pl.BlockSpec(memory_space=pl.ANY), pl.BlockSpec(memory_space=vmem)),
        scratch_shapes=[
            vmem((SNAPS, 2, NX, NY), F32),
            vmem((5, SNAPS, NY), F32),
            vmem((NX + 4, 2, SNAPS, NY), F32),
            vmem((NX + 2, 2, SNAPS, NY), F32),
            vmem((NX, 2, SNAPS, NY), F32),
            vmem((SNAPS, 2, NX, NY), F32),
            vmem((NX, 2, SNAPS, NY), LOW),
            vmem((NX + 8, 2, 2 * SNAPS, NY), LOW),
            vmem((NX + 4, 2, 2 * SNAPS, NY), F32),
            vmem((NX + 2, 2, 2 * SNAPS, NY), F32),
            vmem((2 * NX, 128, NY), LOW),
            vmem((RING, BLOCK, 2, NX, NY), LOW),
            vmem((2 * NX, ADJS, NY), LOW),
            vmem((128, ADJS), F32),
            vmem((ROWS, 16, 128), F32),
            vmem((ROWS, 16, 128), F32),
            vmem((ROWS, 16, 128), F32),
            pltpu.SemaphoreType.DMA((2,)),
            pltpu.SemaphoreType.DMA((RING,)),
            pltpu.SemaphoreType.DMA((4,)),
            pltpu.SemaphoreType.DMA((4,)),
            pltpu.SemaphoreType.DMA((4,)),
            pltpu.SemaphoreType.DMA((4,)),
            pltpu.SemaphoreType.DMA((6,)),
            pltpu.SemaphoreType.DMA((6,)),
            pltpu.SemaphoreType.DMA((2,)),
            pltpu.SemaphoreType.DMA((2,)),
            pltpu.SemaphoreType.DMA((4,)),
        ],
        compiler_params=pltpu.CompilerParams(
            collective_id=0, has_side_effects=True, vmem_limit_bytes=60 * 2**20
        ),
    )(snapshots, adjoint, base_flow.reshape(1, NY), shear.reshape(1, NY))


def solution(mesh):
    in_specs = (P("cols", None, "rows", None), P("cols", None, "rows", None), P(), P())
    out_specs = (P("cols", None, "rows", None), P(None, None, "cols"))
    return jax.shard_map(
        per_device, mesh=mesh, in_specs=in_specs, out_specs=out_specs, check_vma=False
    )
```

```python
import functools

import jax
import jax.numpy as jnp
from jax import lax
from jax.experimental import pallas as pl
from jax.experimental.pallas import tpu as pltpu
from jax.sharding import PartitionSpec as P

ROWS = 32
SNAPS = 16
ADJS = 512
NX = 16
NY = 512
BLOCK = 32
LOADS = ADJS // BLOCK
SCALE = 8192.0
TINY = 1e-37
CUTS = ((2, 6), (8, 4), (12, 4), (16, 2))
OFFSETS = sorted(
    ((dx, dz, dy) for dx in range(4) for dz in range(4) for dy in range(2) if dx or dz or dy),
    key=lambda step: -(min(step[0], 4 - step[0]) + min(step[1], 4 - step[1]) + 2 * step[2]),
)
MESH = pl.DeviceIdType.MESH
NT = (((1,), (1,)), ((), ()))
F32 = jnp.float32
LOW = jnp.bfloat16


def encode(value):
    scaled = value * SCALE
    square = scaled * scaled
    return ((scaled * jnp.abs(scaled)) * (square * (square * square))).astype(LOW)


def decode(code):
    wide = code.astype(F32)
    half = lax.rsqrt(jnp.maximum(jnp.abs(wide), TINY))
    eighth = lax.rsqrt(lax.rsqrt(half))
    return (wide * half) * (eighth * eighth * eighth) * (1.0 / SCALE)


def kernel(
    snaps_hbm, adj_hbm, base_ref, shear_ref,
    adv_hbm, gram_ref,
    snaps, coef, own, own_one, own_adv, adv_out, code, halo_code,
    code_d, code_p, far_d, far_p, one_d, one_p,
    low_own, low_side, low_d, low_p,
    adj_raw, adj, total, part, gather, result,
    io_sem, load_sem, halo_send, halo_recv, far_send, far_recv,
    pass_send, pass_recv, side_send, side_recv, sum_sem,
):
    row = lax.axis_index("rows")
    col = lax.axis_index("cols")
    side = col + 1 - 2 * (col % 2)
    far_col = (col + 2) % 4
    up = (row + 1) % ROWS
    down = (row + ROWS - 1) % ROWS
    here_x, here_z, here_y = row // 8, (row // 2) % 4, row % 2

    def others():
        for dx, dz, dy in OFFSETS:
            yield ((here_x + dx) % 4) * 8 + ((here_z + dz) % 4) * 2 + (here_y + dy) % 2

    def load(i):
        return pltpu.make_async_copy(
            adj_hbm.at[pl.ds(pl.multiple_of(i * BLOCK, BLOCK), BLOCK)],
            adj_raw.at[i],
            load_sem.at[i],
        )

    def send(src, dst, out_sem, in_sem, to_row, to_col):
        return pltpu.make_async_remote_copy(
            src, dst, out_sem, in_sem, device_id=(to_row, to_col), device_id_type=MESH
        )

    snaps_in = pltpu.make_async_copy(snaps_hbm, snaps, io_sem.at[0])
    snaps_in.start()
    for i in range(LOADS):
        load(i).start()

    barrier = pltpu.get_barrier_semaphore()
    for to in others():
        pl.semaphore_signal(barrier, inc=1, device_id=(to, col), device_id_type=MESH)
    for to in ((row, far_col), (row, side), (up, far_col), (down, far_col)):
        pl.semaphore_signal(barrier, inc=1, device_id=to, device_id_type=MESH)

    lane = lax.broadcasted_iota(jnp.int32, (SNAPS, NY), 1)
    base = jnp.broadcast_to(base_ref[...], (SNAPS, NY))
    coef[0] = 0.1 - 0.3 * base
    coef[1] = 0.1 + 0.3 * base
    coef[2] = jnp.where(lane == NY - 1, 0.0, 0.1)
    coef[3] = jnp.where(lane == 0, 0.0, 0.1)
    coef[4] = 0.3 * jnp.broadcast_to(shear_ref[...], (SNAPS, NY))

    snaps_in.wait()
    for c in range(2):
        turned = jnp.swapaxes(snaps[:, c], 0, 1)
        own[pl.ds(2, NX), c] = turned
        code[:, c] = encode(turned)

    pl.semaphore_wait(barrier, ROWS - 1 + 4)

    tail, head = code.at[pl.ds(NX - 2, 2)], code.at[pl.ds(0, 2)]
    halos = [
        send(tail, halo_code.at[pl.ds(0, 2)], halo_send.at[0], halo_recv.at[0], up, col),
        send(head, halo_code.at[pl.ds(2, 2)], halo_send.at[1], halo_recv.at[1], down, col),
        send(tail, code_d.at[pl.ds(0, 2)], halo_send.at[2], halo_recv.at[2], up, far_col),
        send(head, code_d.at[pl.ds(NX + 2, 2)], halo_send.at[3], halo_recv.at[3], down, far_col),
    ]
    fars = [
        send(
            code.at[pl.ds(at - 2, count)], code_d.at[pl.ds(at, count)],
            far_send.at[j], far_recv.at[j], row, far_col,
        )
        for j, (at, count) in enumerate(CUTS)
    ]
    for copy in halos + fars:
        copy.start()

    passes = [
        send(
            code_d.at[pl.ds(at, count)], code_p.at[pl.ds(at, count)],
            pass_send.at[j], pass_recv.at[j], row, side,
        )
        for j, (at, count) in enumerate(CUTS + ((0, 2), (NX + 2, 2)))
    ]

    def turn(i, _):
        load(i).wait()
        for c in range(2):
            block = jnp.swapaxes(adj_raw[i, :, c], 0, 1)
            for x in range(NX):
                adj[2 * x + c, pl.ds(pl.multiple_of(i * BLOCK, BLOCK), BLOCK)] = block[x]
        return 0

    def step(ref, x):
        flow = [ref[x, 0], ref[x, 1]]
        values = []
        for c in range(2):
            here = flow[c]
            value = 0.6 * here + (coef[0] * ref[x + 1, c] + coef[1] * ref[x - 1, c])
            value += coef[2] * pltpu.roll(here, NY - 1, 1) + coef[3] * pltpu.roll(here, 1, 1)
            if c == 0:
                value -= coef[4] * flow[1]
            values.append(value)
        return values

    lax.fori_loop(0, LOADS // 2, turn, 0)

    halos[0].wait_recv()
    halos[1].wait_recv()
    for k in range(2):
        for c in range(2):
            own[k, c] = decode(halo_code[k, c])
            own[NX + 2 + k, c] = decode(halo_code[2 + k, c])

    def own_first(i, _):
        for k in range(3):
            x = 3 * i + k
            values = step(own, x + 1)
            for c in range(2):
                own_one[x, c] = values[c]
        return 0

    lax.fori_loop(0, (NX + 2) // 3, own_first, 0)

    def own_second(i, _):
        for k in range(4):
            x = 4 * i + k
            values = step(own_one, x + 1)
            for c in range(2):
                own_adv[x, c] = values[c]
                low_own[2 * x + c, pl.ds(0, SNAPS)] = own_one[x + 1, c].astype(LOW)
                low_own[2 * x + c, pl.ds(SNAPS, SNAPS)] = values[c].astype(LOW)
        return 0

    lax.fori_loop(0, NX // 4, own_second, 0)
    to_side = send(low_own, low_side, side_send.at[0], side_recv.at[0], row, side)
    to_side.start()

    lax.fori_loop(LOADS // 2, LOADS - 4, turn, 0)
    for k in range(2):
        halos[2 + k].wait_recv()
        passes[4 + k].start()
    fars[0].wait_recv()
    passes[0].start()
    lax.fori_loop(LOADS - 4, LOADS, turn, 0)

    for c in range(2):
        adv_out[:, c] = jnp.swapaxes(own_adv[:, c], 0, 1)
    adv_copy = pltpu.make_async_copy(adv_out, adv_hbm, io_sem.at[1])
    adv_copy.start()

    def states(codes, wide, one, low, j):
        first = 0 if j == 0 else 4 * j + 4
        for k in range(first, 4 * j + 8):
            for c in range(2):
                wide[k, c] = decode(codes[k, c])
        for x in range(0 if j == 0 else 4 * j + 2, 4 * j + 6):
            values = step(wide, x + 1)
            for c in range(2):
                one[x, c] = values[c]
        for x in range(4 * j, 4 * j + 4):
            values = step(one, x + 1)
            for c in range(2):
                low[2 * x + c, pl.ds(0, SNAPS)] = one[x + 1, c].astype(LOW)
                low[2 * x + c, pl.ds(SNAPS, SNAPS)] = values[c].astype(LOW)

    def multiply(at):
        left = jnp.concatenate(
            [
                jnp.concatenate([ref[at + i] for ref in (low_own, low_side, low_d, low_p)], axis=0)
                for i in range(4)
            ],
            axis=1,
        )
        right = jnp.concatenate([adj[at + i] for i in range(4)], axis=1)
        product = lax.dot_general(left, right, NT, preferred_element_type=F32)
        if at == 0:
            total[...] = product
        else:
            total[...] += product

    states(code_d, far_d, one_d, low_d, 0)
    for copy in (passes[4], passes[5], passes[0], to_side):
        copy.wait_recv()
    states(code_p, far_p, one_p, low_p, 0)
    for j in range(1, 4):
        fars[j].wait_recv()
        passes[j].start()
        multiply(8 * j - 8)
        states(code_d, far_d, one_d, low_d, j)
        passes[j].wait_recv()
        multiply(8 * j - 4)
        states(code_p, far_p, one_p, low_p, j)
    multiply(24)
    multiply(28)

    for g in range(8):
        who = (col, side, far_col, (side + 2) % 4)[g // 2]
        for k in range(4):
            part[(4 * (g % 2) + who) * 4 + k] = total[pl.ds(16 * g, 16), pl.ds(128 * k, 128)]

    for to in others():
        send(part.at[to], gather.at[row], sum_sem.at[0], sum_sem.at[1], to, col).start()
    gather[row] = part[row]
    rest = gather.at[pl.ds(0, ROWS - 1)]
    pltpu.make_async_copy(rest, rest, sum_sem.at[1]).wait()
    sums = [gather[t] for t in range(ROWS)]
    while len(sums) > 1:
        sums = [sums[t] + sums[t + 1] for t in range(0, len(sums), 2)]
    result[row] = sums[0]

    for to in others():
        send(result.at[row], result.at[row], sum_sem.at[2], sum_sem.at[3], to, col).start()
    adv_copy.wait()
    for copy in halos + fars + passes + [to_side]:
        copy.wait_send()
    pltpu.make_async_copy(rest, rest, sum_sem.at[0]).wait()
    pltpu.make_async_copy(rest, rest, sum_sem.at[3]).wait()
    for t in range(ROWS):
        at = 16 * (t // 4)
        gram_ref[at // 64, pl.ds(at % 64, 16), pl.ds(128 * (t % 4), 128)] = result[t]
    pltpu.make_async_copy(rest, rest, sum_sem.at[2]).wait()


def per_device(snapshots, adjoint, base_flow, shear):
    vmem = pltpu.VMEM
    return pl.pallas_call(
        kernel,
        out_shape=(
            jax.ShapeDtypeStruct((SNAPS, 2, NX, NY), F32),
            jax.ShapeDtypeStruct((2, 64, ADJS), F32),
        ),
        in_specs=[
            pl.BlockSpec(memory_space=pl.ANY),
            pl.BlockSpec(memory_space=pl.ANY),
            pl.BlockSpec(memory_space=vmem),
            pl.BlockSpec(memory_space=vmem),
        ],
        out_specs=(pl.BlockSpec(memory_space=pl.ANY), pl.BlockSpec(memory_space=vmem)),
        scratch_shapes=[
            vmem((SNAPS, 2, NX, NY), F32),
            vmem((5, SNAPS, NY), F32),
            vmem((NX + 4, 2, SNAPS, NY), F32),
            vmem((NX + 2, 2, SNAPS, NY), F32),
            vmem((NX, 2, SNAPS, NY), F32),
            vmem((SNAPS, 2, NX, NY), F32),
            vmem((NX, 2, SNAPS, NY), LOW),
            vmem((4, 2, SNAPS, NY), LOW),
            vmem((NX + 4, 2, SNAPS, NY), LOW),
            vmem((NX + 4, 2, SNAPS, NY), LOW),
            vmem((NX + 4, 2, SNAPS, NY), F32),
            vmem((NX + 4, 2, SNAPS, NY), F32),
            vmem((NX + 2, 2, SNAPS, NY), F32),
            vmem((NX + 2, 2, SNAPS, NY), F32),
            vmem((2 * NX, 2 * SNAPS, NY), LOW),
            vmem((2 * NX, 2 * SNAPS, NY), LOW),
            vmem((2 * NX, 2 * SNAPS, NY), LOW),
            vmem((2 * NX, 2 * SNAPS, NY), LOW),
            vmem((LOADS, BLOCK, 2, NX, NY), LOW),
            vmem((2 * NX, ADJS, NY), LOW),
            vmem((128, ADJS), F32),
            vmem((ROWS, 16, 128), F32),
            vmem((ROWS, 16, 128), F32),
            vmem((ROWS, 16, 128), F32),
            pltpu.SemaphoreType.DMA((2,)),
            pltpu.SemaphoreType.DMA((LOADS,)),
            pltpu.SemaphoreType.DMA((4,)),
            pltpu.SemaphoreType.DMA((4,)),
            pltpu.SemaphoreType.DMA((4,)),
            pltpu.SemaphoreType.DMA((4,)),
            pltpu.SemaphoreType.DMA((6,)),
            pltpu.SemaphoreType.DMA((6,)),
            pltpu.SemaphoreType.DMA((1,)),
            pltpu.SemaphoreType.DMA((1,)),
            pltpu.SemaphoreType.DMA((4,)),
        ],
        compiler_params=pltpu.CompilerParams(
            collective_id=0, has_side_effects=True, vmem_limit_bytes=60 * 2**20
        ),
    )(snapshots, adjoint, base_flow.reshape(1, NY), shear.reshape(1, NY))


def solution(mesh):
    in_specs = (P("cols", None, "rows", None), P("cols", None, "rows", None), P(), P())
    out_specs = (P("cols", None, "rows", None), P(None, None, "cols"))
    return jax.shard_map(
        per_device, mesh=mesh, in_specs=in_specs, out_specs=out_specs, check_vma=False
    )
```

```python
import functools

import jax
import jax.numpy as jnp
from jax import lax
from jax.experimental import pallas as pl
from jax.experimental.pallas import tpu as pltpu
from jax.sharding import PartitionSpec as P

ROWS = 32
SNAPS = 16
ADJS = 512
NX = 16
NY = 512
BLOCK = 32
LOADS = ADJS // BLOCK
SCALE = 8192.0
TINY = 1e-37
CUTS = ((16, 2), (2, 2), (4, 4), (8, 4), (12, 2), (14, 2))
OFFSETS = sorted(
    ((dx, dz, dy) for dx in range(4) for dz in range(4) for dy in range(2) if dx or dz or dy),
    key=lambda step: -(min(step[0], 4 - step[0]) + min(step[1], 4 - step[1]) + 2 * step[2]),
)
MESH = pl.DeviceIdType.MESH
NT = (((1,), (1,)), ((), ()))
F32 = jnp.float32
LOW = jnp.bfloat16


def encode(value):
    scaled = value * SCALE
    square = scaled * scaled
    return ((scaled * jnp.abs(scaled)) * (square * (square * square))).astype(LOW)


def decode(code):
    wide = code.astype(F32)
    half = lax.rsqrt(jnp.maximum(jnp.abs(wide), TINY))
    eighth = lax.rsqrt(lax.rsqrt(half))
    return (wide * half) * (eighth * eighth * eighth) * (1.0 / SCALE)


def kernel(
    snaps_hbm, adj_hbm, base_ref, shear_ref,
    adv_hbm, gram_hbm,
    snaps, coef, own, own_one, own_adv, adv_out, code, halo_code,
    code_d, code_p, far_d, far_p, one_d, one_p,
    low_own, low_side, low_d, low_p,
    adj_raw, adj, total, part, gather, result,
    io_sem, load_sem, halo_send, halo_recv, far_send, far_recv,
    pass_send, pass_recv, side_send, side_recv, both_send, both_recv, sum_sem,
):
    row = lax.axis_index("rows")
    col = lax.axis_index("cols")
    side = col + 1 - 2 * (col % 2)
    far_col = (col + 2) % 4
    far_side = (side + 2) % 4
    up = (row + 1) % ROWS
    down = (row + ROWS - 1) % ROWS
    here_x, here_z, here_y = row // 8, (row // 2) % 4, row % 2

    def others():
        for dx, dz, dy in OFFSETS:
            yield ((here_x + dx) % 4) * 8 + ((here_z + dz) % 4) * 2 + (here_y + dy) % 2

    def load(i):
        return pltpu.make_async_copy(
            adj_hbm.at[pl.ds(pl.multiple_of(i * BLOCK, BLOCK), BLOCK)],
            adj_raw.at[i],
            load_sem.at[i],
        )

    def send(src, dst, out_sem, in_sem, to_row, to_col):
        return pltpu.make_async_remote_copy(
            src, dst, out_sem, in_sem, device_id=(to_row, to_col), device_id_type=MESH
        )

    snaps_in = pltpu.make_async_copy(snaps_hbm, snaps, io_sem.at[0])
    snaps_in.start()
    for i in range(LOADS):
        load(i).start()

    barrier = pltpu.get_barrier_semaphore()
    for to in others():
        pl.semaphore_signal(barrier, inc=1, device_id=(to, col), device_id_type=MESH)
    for to in ((row, far_col), (row, side), (row, far_side), (up, far_col), (down, far_col)):
        pl.semaphore_signal(barrier, inc=1, device_id=to, device_id_type=MESH)

    lane = lax.broadcasted_iota(jnp.int32, (SNAPS, NY), 1)
    base = jnp.broadcast_to(base_ref[...], (SNAPS, NY))
    coef[0] = 0.1 - 0.3 * base
    coef[1] = 0.1 + 0.3 * base
    coef[2] = jnp.where(lane == NY - 1, 0.0, 0.1)
    coef[3] = jnp.where(lane == 0, 0.0, 0.1)
    coef[4] = 0.3 * jnp.broadcast_to(shear_ref[...], (SNAPS, NY))

    snaps_in.wait()
    for c in range(2):
        turned = jnp.swapaxes(snaps[:, c], 0, 1)
        own[pl.ds(2, NX), c] = turned
        code[:, c] = encode(turned)

    pl.semaphore_wait(barrier, ROWS - 1 + 5)

    fars = [
        send(
            code.at[pl.ds(at - 2, count)], code_d.at[pl.ds(at, count)],
            far_send.at[j], far_recv.at[j], row, far_col,
        )
        for j, (at, count) in enumerate(CUTS)
    ]
    at, count = CUTS[-1]
    both = send(
        code.at[pl.ds(at - 2, count)], code_p.at[pl.ds(at, count)],
        both_send.at[0], both_recv.at[0], row, far_side,
    )
    halos = [
        send(code.at[pl.ds(NX - 2, 2)], code_d.at[pl.ds(0, 2)],
             halo_send.at[0], halo_recv.at[0], up, far_col),
        send(code.at[pl.ds(0, 2)], code_d.at[pl.ds(NX + 2, 2)],
             halo_send.at[1], halo_recv.at[1], down, far_col),
    ]
    for copy in [fars[0], fars[1]] + halos + fars[2:] + [both]:
        copy.start()
    relays = [
        send(code_d.at[pl.ds(NX, 2)], halo_code.at[pl.ds(0, 2)],
             halo_send.at[2], halo_recv.at[2], up, far_col),
        send(code_d.at[pl.ds(2, 2)], halo_code.at[pl.ds(2, 2)],
             halo_send.at[3], halo_recv.at[3], down, far_col),
    ]
    passes = [
        send(
            code_d.at[pl.ds(at, count)], code_p.at[pl.ds(at, count)],
            pass_send.at[j], pass_recv.at[j], row, side,
        )
        for j, (at, count) in enumerate(CUTS[:-1] + ((0, 2), (NX + 2, 2)))
    ]

    def turn(i, _):
        load(i).wait()
        for c in range(2):
            block = jnp.swapaxes(adj_raw[i, :, c], 0, 1)
            for x in range(NX):
                adj[2 * x + c, pl.ds(pl.multiple_of(i * BLOCK, BLOCK), BLOCK)] = block[x]
        return 0

    def step(ref, x):
        flow = [ref[x, 0], ref[x, 1]]
        values = []
        for c in range(2):
            here = flow[c]
            value = 0.6 * here + (coef[0] * ref[x + 1, c] + coef[1] * ref[x - 1, c])
            value += coef[2] * pltpu.roll(here, NY - 1, 1) + coef[3] * pltpu.roll(here, 1, 1)
            if c == 0:
                value -= coef[4] * flow[1]
            values.append(value)
        return values

    def own_first(x):
        values = step(own, x + 1)
        for c in range(2):
            own_one[x, c] = values[c]

    def own_second(x):
        values = step(own_one, x + 1)
        for c in range(2):
            own_adv[x, c] = values[c]
            low_own[2 * x + c, pl.ds(0, SNAPS)] = own_one[x + 1, c].astype(LOW)
            low_own[2 * x + c, pl.ds(SNAPS, SNAPS)] = values[c].astype(LOW)

    def inner_first(i, _):
        for k in range(2):
            own_first(2 * i + k)
        return 0

    def inner_second(i, _):
        for k in range(4):
            own_second(2 + 4 * i + k)
        return 0

    lax.fori_loop(1, NX // 2, inner_first, 0)
    lax.fori_loop(0, 3, inner_second, 0)
    to_side = [
        send(low_own.at[pl.ds(at, count)], low_side.at[pl.ds(at, count)],
             side_send.at[j], side_recv.at[j], row, side)
        for j, (at, count) in enumerate(((4, 24), (0, 4), (28, 4)))
    ]
    to_side[0].start()

    lax.fori_loop(0, 5, turn, 0)
    for k in range(2):
        fars[k].wait_recv()
        relays[k].start()
        passes[k].start()
        lax.fori_loop(5 + 2 * k, 7 + 2 * k, turn, 0)
    for k in range(2):
        halos[k].wait_recv()
        passes[5 + k].start()
    lax.fori_loop(9, LOADS, turn, 0)

    relays[0].wait_recv()
    relays[1].wait_recv()
    for k in range(2):
        for c in range(2):
            own[k, c] = decode(halo_code[k, c])
            own[NX + 2 + k, c] = decode(halo_code[2 + k, c])
    for x in (0, 1, NX, NX + 1):
        own_first(x)
    for x in (0, 1, NX - 2, NX - 1):
        own_second(x)
    to_side[1].start()
    to_side[2].start()

    fars[2].wait_recv()
    passes[2].start()
    for c in range(2):
        adv_out[:, c] = jnp.swapaxes(own_adv[:, c], 0, 1)
    adv_copy = pltpu.make_async_copy(adv_out, adv_hbm, io_sem.at[1])
    adv_copy.start()

    def states(refs, codes, firsts, seconds):
        code_ref, wide, one, low = refs
        for k in codes:
            for c in range(2):
                wide[k, c] = decode(code_ref[k, c])
        for x in firsts:
            values = step(wide, x + 1)
            for c in range(2):
                one[x, c] = values[c]
        for x in seconds:
            values = step(one, x + 1)
            for c in range(2):
                low[2 * x + c, pl.ds(0, SNAPS)] = one[x + 1, c].astype(LOW)
                low[2 * x + c, pl.ds(SNAPS, SNAPS)] = values[c].astype(LOW)

    direct = (code_d, far_d, one_d, low_d)
    passed = (code_p, far_p, one_p, low_p)

    def multiply(at):
        left = jnp.concatenate(
            [
                jnp.concatenate([ref[at + i] for ref in (low_own, low_side, low_d, low_p)], axis=0)
                for i in range(4)
            ],
            axis=1,
        )
        right = jnp.concatenate([adj[at + i] for i in range(4)], axis=1)
        product = lax.dot_general(left, right, NT, preferred_element_type=F32)
        if at == 4:
            total[...] = product
        else:
            total[...] += product

    states(direct, range(8), range(6), range(4))
    for copy in (passes[5], passes[1], passes[2]):
        copy.wait_recv()
    states(passed, range(8), range(6), range(4))

    to_side[0].wait_recv()
    fars[3].wait_recv()
    passes[3].start()
    multiply(4)
    states(direct, range(8, 12), range(6, 10), range(4, 8))
    passes[3].wait_recv()
    to_side[1].wait_recv()
    multiply(0)
    states(passed, range(8, 12), range(6, 10), range(4, 8))

    fars[4].wait_recv()
    passes[4].start()
    for copy in (passes[0], passes[6]):
        copy.wait_recv()
    multiply(8)
    states(direct, (12, 13, 16, 17, 18, 19), (10, 11, 16, 17), (8, 9))
    passes[4].wait_recv()
    multiply(12)
    states(passed, (12, 13, 16, 17, 18, 19), (10, 11, 16, 17), (8, 9))

    fars[5].wait_recv()
    multiply(16)
    states(direct, (14, 15), range(12, 16), range(10, 16))
    both.wait_recv()
    to_side[2].wait_recv()
    states(passed, (14, 15), range(12, 16), range(10, 16))
    multiply(20)
    multiply(24)
    multiply(28)

    for g in range(8):
        who = (col, side, far_col, far_side)[g // 2]
        for k in range(4):
            part[(4 * (g % 2) + who) * 4 + k] = total[pl.ds(16 * g, 16), pl.ds(128 * k, 128)]

    for to in others():
        send(part.at[to], gather.at[row], sum_sem.at[0], sum_sem.at[1], to, col).start()
    gather[row] = part[row]
    rest = gather.at[pl.ds(0, ROWS - 1)]
    pltpu.make_async_copy(rest, rest, sum_sem.at[1]).wait()
    sums = [gather[t] for t in range(ROWS)]
    while len(sums) > 1:
        sums = [sums[t] + sums[t + 1] for t in range(0, len(sums), 2)]
    result[...] = sums[0]

    place = gram_hbm.at[
        row // 16,
        pl.ds(pl.multiple_of((row // 4) % 4 * 16, 16), 16),
        pl.ds(pl.multiple_of(row % 4 * 128, 128), 128),
    ]
    for to in others():
        send(result, place, sum_sem.at[2], sum_sem.at[3], to, col).start()
    own_piece = pltpu.make_async_copy(result, place, io_sem.at[0])
    own_piece.start()
    adv_copy.wait()
    for copy in halos + fars + relays + passes + to_side + [both]:
        copy.wait_send()
    own_piece.wait()
    pltpu.make_async_copy(rest, rest, sum_sem.at[0]).wait()
    pltpu.make_async_copy(rest, rest, sum_sem.at[2]).wait()
    pltpu.make_async_copy(rest, rest, sum_sem.at[3]).wait()


def hand_on(adv_in, gram_in, adv_hbm, gram_hbm, adv, gram, in_sem, out_sem):
    ways = [(adv_in.at[pl.ds(4 * i, 4)], adv.at[pl.ds(4 * i, 4)], adv_hbm.at[pl.ds(4 * i, 4)]) for i in range(4)]
    ways += [(gram_in.at[i], gram.at[i], gram_hbm.at[i]) for i in range(2)]
    for i, (src, mid, _) in enumerate(ways):
        pltpu.make_async_copy(src, mid, in_sem.at[i]).start()
    for i, (src, mid, dst) in enumerate(ways):
        pltpu.make_async_copy(src, mid, in_sem.at[i]).wait()
        pltpu.make_async_copy(mid, dst, out_sem.at[i]).start()
    for i, (_, mid, dst) in enumerate(ways):
        pltpu.make_async_copy(mid, dst, out_sem.at[i]).wait()


def per_device(snapshots, adjoint, base_flow, shear):
    vmem = pltpu.VMEM
    somewhere = pl.BlockSpec(memory_space=pl.ANY)
    shapes = (
        jax.ShapeDtypeStruct((SNAPS, 2, NX, NY), F32),
        jax.ShapeDtypeStruct((2, 64, ADJS), F32),
    )
    results = pl.pallas_call(
        kernel,
        out_shape=shapes,
        in_specs=[
            somewhere,
            somewhere,
            pl.BlockSpec(memory_space=vmem),
            pl.BlockSpec(memory_space=vmem),
        ],
        out_specs=(somewhere, somewhere),
        scratch_shapes=[
            vmem((SNAPS, 2, NX, NY), F32),
            vmem((5, SNAPS, NY), F32),
            vmem((NX + 4, 2, SNAPS, NY), F32),
            vmem((NX + 2, 2, SNAPS, NY), F32),
            vmem((NX, 2, SNAPS, NY), F32),
            vmem((SNAPS, 2, NX, NY), F32),
            vmem((NX, 2, SNAPS, NY), LOW),
            vmem((4, 2, SNAPS, NY), LOW),
            vmem((NX + 4, 2, SNAPS, NY), LOW),
            vmem((NX + 4, 2, SNAPS, NY), LOW),
            vmem((NX + 4, 2, SNAPS, NY), F32),
            vmem((NX + 4, 2, SNAPS, NY), F32),
            vmem((NX + 2, 2, SNAPS, NY), F32),
            vmem((NX + 2, 2, SNAPS, NY), F32),
            vmem((2 * NX, 2 * SNAPS, NY), LOW),
            vmem((2 * NX, 2 * SNAPS, NY), LOW),
            vmem((2 * NX, 2 * SNAPS, NY), LOW),
            vmem((2 * NX, 2 * SNAPS, NY), LOW),
            vmem((LOADS, BLOCK, 2, NX, NY), LOW),
            vmem((2 * NX, ADJS, NY), LOW),
            vmem((128, ADJS), F32),
            vmem((ROWS, 16, 128), F32),
            vmem((ROWS, 16, 128), F32),
            vmem((16, 128), F32),
            pltpu.SemaphoreType.DMA((2,)),
            pltpu.SemaphoreType.DMA((LOADS,)),
            pltpu.SemaphoreType.DMA((4,)),
            pltpu.SemaphoreType.DMA((4,)),
            pltpu.SemaphoreType.DMA((6,)),
            pltpu.SemaphoreType.DMA((6,)),
            pltpu.SemaphoreType.DMA((7,)),
            pltpu.SemaphoreType.DMA((7,)),
            pltpu.SemaphoreType.DMA((3,)),
            pltpu.SemaphoreType.DMA((3,)),
            pltpu.SemaphoreType.DMA((1,)),
            pltpu.SemaphoreType.DMA((1,)),
            pltpu.SemaphoreType.DMA((4,)),
        ],
        compiler_params=pltpu.CompilerParams(
            collective_id=0, has_side_effects=True, vmem_limit_bytes=60 * 2**20
        ),
    )(snapshots, adjoint, base_flow.reshape(1, NY), shear.reshape(1, NY))
    return pl.pallas_call(
        hand_on,
        out_shape=shapes,
        in_specs=[somewhere, somewhere],
        out_specs=(somewhere, somewhere),
        scratch_shapes=[
            vmem((SNAPS, 2, NX, NY), F32),
            vmem((2, 64, ADJS), F32),
            pltpu.SemaphoreType.DMA((6,)),
            pltpu.SemaphoreType.DMA((6,)),
        ],
    )(*results)


def solution(mesh):
    in_specs = (P("cols", None, "rows", None), P("cols", None, "rows", None), P(), P())
    out_specs = (P("cols", None, "rows", None), P(None, None, "cols"))
    return jax.shard_map(
        per_device, mesh=mesh, in_specs=in_specs, out_specs=out_specs, check_vma=False
    )
```

```python
import functools

import jax
import jax.numpy as jnp
from jax import lax
from jax.experimental import pallas as pl
from jax.experimental.pallas import tpu as pltpu
from jax.sharding import PartitionSpec as P

ROWS = 32
SNAPS = 16
ADJS = 512
NX = 16
NY = 512
BLOCK = 32
LOADS = ADJS // BLOCK
TURNED = 20
SCALE = 8192.0
TINY = 1e-37
CUTS = ((16, 2), (2, 2), (4, 4), (8, 4), (12, 2), (14, 2))
OFFSETS = sorted(
    ((dx, dz, dy) for dx in range(4) for dz in range(4) for dy in range(2) if dx or dz or dy),
    key=lambda step: -(min(step[0], 4 - step[0]) + min(step[1], 4 - step[1]) + 2 * step[2]),
)
MESH = pl.DeviceIdType.MESH
NT = (((1,), (1,)), ((), ()))
F32 = jnp.float32
LOW = jnp.bfloat16


def encode(value):
    scaled = value * SCALE
    square = scaled * scaled
    return ((scaled * jnp.abs(scaled)) * (square * (square * square))).astype(LOW)


def decode(code):
    wide = code.astype(F32)
    half = lax.rsqrt(jnp.maximum(jnp.abs(wide), TINY))
    eighth = lax.rsqrt(lax.rsqrt(half))
    return (wide * half) * (eighth * eighth * eighth) * (1.0 / SCALE)


def kernel(
    snaps_hbm, adj_hbm, base_ref, shear_ref,
    adv_hbm, gram_hbm,
    snaps, coef, own, own_one, own_adv, adv_out, code, halo_code,
    code_d, code_p, far_d, far_p, one_d, one_p,
    low_own, low_side, low_d, low_p,
    adj_raw, adj, adj_t, total, part, gather, result,
    io_sem, load_sem, halo_send, halo_recv, far_send, far_recv,
    pass_send, pass_recv, side_send, side_recv, both_send, both_recv, sum_sem,
):
    row = lax.axis_index("rows")
    col = lax.axis_index("cols")
    side = col + 1 - 2 * (col % 2)
    far_col = (col + 2) % 4
    far_side = (side + 2) % 4
    up = (row + 1) % ROWS
    down = (row + ROWS - 1) % ROWS
    here_x, here_z, here_y = row // 8, (row // 2) % 4, row % 2

    def others():
        for dx, dz, dy in OFFSETS:
            yield ((here_x + dx) % 4) * 8 + ((here_z + dz) % 4) * 2 + (here_y + dy) % 2

    def load(i):
        return pltpu.make_async_copy(
            adj_hbm.at[pl.ds(pl.multiple_of(i * BLOCK, BLOCK), BLOCK)],
            adj_raw.at[i],
            load_sem.at[i],
        )

    def send(src, dst, out_sem, in_sem, to_row, to_col):
        return pltpu.make_async_remote_copy(
            src, dst, out_sem, in_sem, device_id=(to_row, to_col), device_id_type=MESH
        )

    snaps_in = pltpu.make_async_copy(snaps_hbm, snaps, io_sem.at[0])
    snaps_in.start()

    barrier = pltpu.get_barrier_semaphore()
    for to in others():
        pl.semaphore_signal(barrier, inc=1, device_id=(to, col), device_id_type=MESH)
    for to in ((row, far_col), (row, side), (row, far_side), (up, far_col), (down, far_col)):
        pl.semaphore_signal(barrier, inc=1, device_id=to, device_id_type=MESH)

    lane = lax.broadcasted_iota(jnp.int32, (SNAPS, NY), 1)
    base = jnp.broadcast_to(base_ref[...], (SNAPS, NY))
    coef[0] = 0.1 - 0.3 * base
    coef[1] = 0.1 + 0.3 * base
    coef[2] = jnp.where(lane == NY - 1, 0.0, 0.1)
    coef[3] = jnp.where(lane == 0, 0.0, 0.1)
    coef[4] = 0.3 * jnp.broadcast_to(shear_ref[...], (SNAPS, NY))

    snaps_in.wait()
    for i in range(LOADS):
        load(i).start()
    for c in range(2):
        turned = jnp.swapaxes(snaps[:, c], 0, 1)
        own[pl.ds(2, NX), c] = turned
        code[:, c] = encode(turned)

    pl.semaphore_wait(barrier, ROWS - 1 + 5)

    fars = [
        send(
            code.at[pl.ds(at - 2, count)], code_d.at[pl.ds(at, count)],
            far_send.at[j], far_recv.at[j], row, far_col,
        )
        for j, (at, count) in enumerate(CUTS)
    ]
    at, count = CUTS[-1]
    both = send(
        code.at[pl.ds(at - 2, count)], code_p.at[pl.ds(at, count)],
        both_send.at[0], both_recv.at[0], row, far_side,
    )
    halos = [
        send(code.at[pl.ds(NX - 2, 2)], code_d.at[pl.ds(0, 2)],
             halo_send.at[0], halo_recv.at[0], up, far_col),
        send(code.at[pl.ds(0, 2)], code_d.at[pl.ds(NX + 2, 2)],
             halo_send.at[1], halo_recv.at[1], down, far_col),
    ]
    for copy in [fars[0], fars[1]] + halos + fars[2:] + [both]:
        copy.start()
    relays = [
        send(code_d.at[pl.ds(NX, 2)], halo_code.at[pl.ds(0, 2)],
             halo_send.at[2], halo_recv.at[2], up, far_col),
        send(code_d.at[pl.ds(2, 2)], halo_code.at[pl.ds(2, 2)],
             halo_send.at[3], halo_recv.at[3], down, far_col),
    ]
    passes = [
        send(
            code_d.at[pl.ds(at, count)], code_p.at[pl.ds(at, count)],
            pass_send.at[j], pass_recv.at[j], row, side,
        )
        for j, (at, count) in enumerate(CUTS[:-1] + ((0, 2), (NX + 2, 2)))
    ]

    def turn(i, _):
        load(i).wait()
        for c in range(2):
            block = jnp.swapaxes(adj_raw[i, :, c], 0, 1)
            for x in range(NX):
                adj[2 * x + c, pl.ds(pl.multiple_of(i * BLOCK, BLOCK), BLOCK)] = block[x]
        return 0

    def turn_group(g):
        lax.fori_loop(4 * g, 4 * g + 4, turn, 0)

        def turn_round(k, _):
            adj_t[k, :, pl.ds(128 * g, 128)] = adj[TURNED + k, pl.ds(128 * g, 128)].T
            return 0

        lax.fori_loop(0, 2 * NX - TURNED, turn_round, 0)

    def step(ref, x):
        flow = [ref[x, 0], ref[x, 1]]
        values = []
        for c in range(2):
            here = flow[c]
            value = 0.6 * here + (coef[0] * ref[x + 1, c] + coef[1] * ref[x - 1, c])
            value += coef[2] * pltpu.roll(here, NY - 1, 1) + coef[3] * pltpu.roll(here, 1, 1)
            if c == 0:
                value -= coef[4] * flow[1]
            values.append(value)
        return values

    def own_first(x):
        values = step(own, x + 1)
        for c in range(2):
            own_one[x, c] = values[c]

    def own_second(x):
        values = step(own_one, x + 1)
        for c in range(2):
            own_adv[x, c] = values[c]
            low_own[2 * x + c, pl.ds(0, SNAPS)] = own_one[x + 1, c].astype(LOW)
            low_own[2 * x + c, pl.ds(SNAPS, SNAPS)] = values[c].astype(LOW)

    def inner_first(i, _):
        for k in range(2):
            own_first(2 * i + k)
        return 0

    def inner_second(i, _):
        for k in range(4):
            own_second(2 + 4 * i + k)
        return 0

    lax.fori_loop(1, NX // 2, inner_first, 0)
    lax.fori_loop(0, 3, inner_second, 0)
    to_side = [
        send(low_own.at[pl.ds(at, count)], low_side.at[pl.ds(at, count)],
             side_send.at[j], side_recv.at[j], row, side)
        for j, (at, count) in enumerate(((4, 24), (0, 4), (28, 4)))
    ]
    to_side[0].start()

    turn_group(0)
    for k in range(2):
        fars[k].wait_recv()
        relays[k].start()
        passes[k].start()
    turn_group(1)
    for k in range(2):
        halos[k].wait_recv()
        passes[5 + k].start()
    turn_group(2)
    fars[2].wait_recv()
    passes[2].start()
    turn_group(3)

    def states(refs, codes, firsts, seconds):
        code_ref, wide, one, low = refs
        for k in codes:
            for c in range(2):
                wide[k, c] = decode(code_ref[k, c])
        for x in firsts:
            values = step(wide, x + 1)
            for c in range(2):
                one[x, c] = values[c]
        for x in seconds:
            values = step(one, x + 1)
            for c in range(2):
                low[2 * x + c, pl.ds(0, SNAPS)] = one[x + 1, c].astype(LOW)
                low[2 * x + c, pl.ds(SNAPS, SNAPS)] = values[c].astype(LOW)

    direct = (code_d, far_d, one_d, low_d)
    passed = (code_p, far_p, one_p, low_p)

    def multiply(at, count=4):
        left = jnp.concatenate(
            [
                jnp.concatenate([ref[at + i] for ref in (low_own, low_side, low_d, low_p)], axis=0)
                for i in range(count)
            ],
            axis=1,
        )
        if at < TURNED:
            right = jnp.concatenate([adj[at + i] for i in range(count)], axis=1)
            product = lax.dot_general(left, right, NT, preferred_element_type=F32)
        else:
            right = adj_t[pl.ds(at - TURNED, count)].reshape(count * NY, ADJS)
            product = jnp.dot(left, right, preferred_element_type=F32)
        if at == 4:
            total[...] = product
        else:
            total[...] += product

    states(direct, range(8), range(6), range(4))
    fars[3].wait_recv()
    passes[3].start()
    for copy in (passes[5], passes[1], passes[2]):
        copy.wait_recv()
    states(passed, range(8), range(6), range(4))
    fars[4].wait_recv()
    passes[4].start()

    relays[0].wait_recv()
    relays[1].wait_recv()
    for k in range(2):
        for c in range(2):
            own[k, c] = decode(halo_code[k, c])
            own[NX + 2 + k, c] = decode(halo_code[2 + k, c])
    for x in (0, 1, NX, NX + 1):
        own_first(x)
    for x in (0, 1, NX - 2, NX - 1):
        own_second(x)
    to_side[1].start()
    to_side[2].start()

    to_side[0].wait_recv()
    multiply(4)
    states(direct, range(8, 12), range(6, 10), range(4, 8))
    passes[3].wait_recv()
    states(passed, range(8, 12), range(6, 10), range(4, 8))

    for copy in (passes[0], passes[6]):
        copy.wait_recv()
    multiply(8)
    states(direct, (12, 13, 16, 17, 18, 19), (10, 11, 16, 17), (8, 9))
    passes[4].wait_recv()
    multiply(12)
    states(passed, (12, 13, 16, 17, 18, 19), (10, 11, 16, 17), (8, 9))
    to_side[1].wait_recv()
    multiply(0)

    fars[5].wait_recv()
    multiply(16)
    states(direct, (14, 15), range(12, 16), range(10, 16))
    both.wait_recv()
    to_side[2].wait_recv()
    states(passed, (14, 15), range(12, 16), range(10, 16))
    multiply(20, 12)

    for g in range(8):
        who = (col, side, far_col, far_side)[g // 2]
        for k in range(4):
            part[(4 * (g % 2) + who) * 4 + k] = total[pl.ds(16 * g, 16), pl.ds(128 * k, 128)]

    for to in others():
        send(part.at[to], gather.at[row], sum_sem.at[0], sum_sem.at[1], to, col).start()
    gather[row] = part[row]
    for c in range(2):
        adv_out[:, c] = jnp.swapaxes(own_adv[:, c], 0, 1)
    adv_copy = pltpu.make_async_copy(adv_out, adv_hbm, io_sem.at[1])
    adv_copy.start()
    rest = gather.at[pl.ds(0, ROWS - 1)]
    pltpu.make_async_copy(rest, rest, sum_sem.at[1]).wait()
    sums = [gather[t] for t in range(ROWS)]
    while len(sums) > 1:
        sums = [sums[t] + sums[t + 1] for t in range(0, len(sums), 2)]
    result[...] = sums[0]

    place = gram_hbm.at[
        row // 16,
        pl.ds(pl.multiple_of((row // 4) % 4 * 16, 16), 16),
        pl.ds(pl.multiple_of(row % 4 * 128, 128), 128),
    ]
    for to in others():
        send(result, place, sum_sem.at[2], sum_sem.at[3], to, col).start()
    own_piece = pltpu.make_async_copy(result, place, io_sem.at[0])
    own_piece.start()
    adv_copy.wait()
    for copy in halos + fars + relays + passes + to_side + [both]:
        copy.wait_send()
    own_piece.wait()
    pltpu.make_async_copy(rest, rest, sum_sem.at[0]).wait()
    pltpu.make_async_copy(rest, rest, sum_sem.at[2]).wait()
    pltpu.make_async_copy(rest, rest, sum_sem.at[3]).wait()


def hand_on(adv_in, gram_in, adv_hbm, gram_hbm, adv, gram, in_sem, out_sem):
    ways = [(adv_in.at[pl.ds(4 * i, 4)], adv.at[pl.ds(4 * i, 4)], adv_hbm.at[pl.ds(4 * i, 4)]) for i in range(4)]
    ways += [(gram_in.at[i], gram.at[i], gram_hbm.at[i]) for i in range(2)]
    for i, (src, mid, _) in enumerate(ways):
        pltpu.make_async_copy(src, mid, in_sem.at[i]).start()
    for i, (src, mid, dst) in enumerate(ways):
        pltpu.make_async_copy(src, mid, in_sem.at[i]).wait()
        pltpu.make_async_copy(mid, dst, out_sem.at[i]).start()
    for i, (_, mid, dst) in enumerate(ways):
        pltpu.make_async_copy(mid, dst, out_sem.at[i]).wait()


def per_device(snapshots, adjoint, base_flow, shear):
    vmem = pltpu.VMEM
    somewhere = pl.BlockSpec(memory_space=pl.ANY)
    shapes = (
        jax.ShapeDtypeStruct((SNAPS, 2, NX, NY), F32),
        jax.ShapeDtypeStruct((2, 64, ADJS), F32),
    )
    results = pl.pallas_call(
        kernel,
        out_shape=shapes,
        in_specs=[
            somewhere,
            somewhere,
            pl.BlockSpec(memory_space=vmem),
            pl.BlockSpec(memory_space=vmem),
        ],
        out_specs=(somewhere, somewhere),
        scratch_shapes=[
            vmem((SNAPS, 2, NX, NY), F32),
            vmem((5, SNAPS, NY), F32),
            vmem((NX + 4, 2, SNAPS, NY), F32),
            vmem((NX + 2, 2, SNAPS, NY), F32),
            vmem((NX, 2, SNAPS, NY), F32),
            vmem((SNAPS, 2, NX, NY), F32),
            vmem((NX, 2, SNAPS, NY), LOW),
            vmem((4, 2, SNAPS, NY), LOW),
            vmem((NX + 4, 2, SNAPS, NY), LOW),
            vmem((NX + 4, 2, SNAPS, NY), LOW),
            vmem((NX + 4, 2, SNAPS, NY), F32),
            vmem((NX + 4, 2, SNAPS, NY), F32),
            vmem((NX + 2, 2, SNAPS, NY), F32),
            vmem((NX + 2, 2, SNAPS, NY), F32),
            vmem((2 * NX, 2 * SNAPS, NY), LOW),
            vmem((2 * NX, 2 * SNAPS, NY), LOW),
            vmem((2 * NX, 2 * SNAPS, NY), LOW),
            vmem((2 * NX, 2 * SNAPS, NY), LOW),
            vmem((LOADS, BLOCK, 2, NX, NY), LOW),
            vmem((2 * NX, ADJS, NY), LOW),
            vmem((2 * NX - TURNED, NY, ADJS), LOW),
            vmem((128, ADJS), F32),
            vmem((ROWS, 16, 128), F32),
            vmem((ROWS, 16, 128), F32),
            vmem((16, 128), F32),
            pltpu.SemaphoreType.DMA((2,)),
            pltpu.SemaphoreType.DMA((LOADS,)),
            pltpu.SemaphoreType.DMA((4,)),
            pltpu.SemaphoreType.DMA((4,)),
            pltpu.SemaphoreType.DMA((6,)),
            pltpu.SemaphoreType.DMA((6,)),
            pltpu.SemaphoreType.DMA((7,)),
            pltpu.SemaphoreType.DMA((7,)),
            pltpu.SemaphoreType.DMA((3,)),
            pltpu.SemaphoreType.DMA((3,)),
            pltpu.SemaphoreType.DMA((1,)),
            pltpu.SemaphoreType.DMA((1,)),
            pltpu.SemaphoreType.DMA((4,)),
        ],
        compiler_params=pltpu.CompilerParams(
            collective_id=0, has_side_effects=True, vmem_limit_bytes=60 * 2**20
        ),
    )(snapshots, adjoint, base_flow.reshape(1, NY), shear.reshape(1, NY))
    return pl.pallas_call(
        hand_on,
        out_shape=shapes,
        in_specs=[somewhere, somewhere],
        out_specs=(somewhere, somewhere),
        scratch_shapes=[
            vmem((SNAPS, 2, NX, NY), F32),
            vmem((2, 64, ADJS), F32),
            pltpu.SemaphoreType.DMA((6,)),
            pltpu.SemaphoreType.DMA((6,)),
        ],
    )(*results)


def solution(mesh):
    in_specs = (P("cols", None, "rows", None), P("cols", None, "rows", None), P(), P())
    out_specs = (P("cols", None, "rows", None), P(None, None, "cols"))
    return jax.shard_map(
        per_device, mesh=mesh, in_specs=in_specs, out_specs=out_specs, check_vma=False
    )
```

```python
import functools

import jax
import jax.numpy as jnp
from jax import lax
from jax.experimental import pallas as pl
from jax.experimental.pallas import tpu as pltpu
from jax.sharding import PartitionSpec as P

ROWS = 32
SNAPS = 16
ADJS = 512
NX = 16
NY = 512
BLOCK = 32
LOADS = ADJS // BLOCK
TURNED = 24
SCALE = 8192.0
TINY = 1e-37
CUTS = ((16, 2), (2, 2), (4, 4), (8, 4), (12, 2), (14, 2))
OFFSETS = sorted(
    ((dx, dz, dy) for dx in range(4) for dz in range(4) for dy in range(2) if dx or dz or dy),
    key=lambda step: -(min(step[0], 4 - step[0]) + min(step[1], 4 - step[1]) + 2 * step[2]),
)
MESH = pl.DeviceIdType.MESH
NT = (((1,), (1,)), ((), ()))
F32 = jnp.float32
LOW = jnp.bfloat16


def encode(value):
    scaled = value * SCALE
    square = scaled * scaled
    return ((scaled * jnp.abs(scaled)) * (square * (square * square))).astype(LOW)


def decode(code):
    wide = code.astype(F32)
    half = lax.rsqrt(jnp.maximum(jnp.abs(wide), TINY))
    eighth = lax.rsqrt(lax.rsqrt(half))
    return (wide * half) * (eighth * eighth * eighth) * (1.0 / SCALE)


def kernel(
    snaps_hbm, adj_hbm, base_ref, shear_ref,
    adv_hbm, gram_hbm,
    snaps, coef, own, own_one, own_adv, adv_out, code, halo_code,
    code_d, code_p, far_d, far_p, one_d, one_p,
    low_own, low_side, low_d, low_p,
    adj_raw, adj, adj_t, total, part, gather, result,
    io_sem, load_sem, halo_send, halo_recv, far_send, far_recv,
    pass_send, pass_recv, side_send, side_recv, both_send, both_recv, sum_sem,
):
    row = lax.axis_index("rows")
    col = lax.axis_index("cols")
    side = col + 1 - 2 * (col % 2)
    far_col = (col + 2) % 4
    far_side = (side + 2) % 4
    up = (row + 1) % ROWS
    down = (row + ROWS - 1) % ROWS
    here_x, here_z, here_y = row // 8, (row // 2) % 4, row % 2

    def others():
        for dx, dz, dy in OFFSETS:
            yield ((here_x + dx) % 4) * 8 + ((here_z + dz) % 4) * 2 + (here_y + dy) % 2

    def load(i):
        return pltpu.make_async_copy(
            adj_hbm.at[pl.ds(pl.multiple_of(i * BLOCK, BLOCK), BLOCK)],
            adj_raw.at[i],
            load_sem.at[i],
        )

    def send(src, dst, out_sem, in_sem, to_row, to_col):
        return pltpu.make_async_remote_copy(
            src, dst, out_sem, in_sem, device_id=(to_row, to_col), device_id_type=MESH
        )

    snaps_in = [
        pltpu.make_async_copy(snaps_hbm.at[:, pl.ds(c, 1)], snaps.at[:, pl.ds(c, 1)], io_sem.at[c])
        for c in range(2)
    ]
    for copy in snaps_in:
        copy.start()

    barrier = pltpu.get_barrier_semaphore()
    for to in others():
        pl.semaphore_signal(barrier, inc=1, device_id=(to, col), device_id_type=MESH)
    for to in ((row, far_col), (row, side), (row, far_side), (up, far_col), (down, far_col)):
        pl.semaphore_signal(barrier, inc=1, device_id=to, device_id_type=MESH)

    lane = lax.broadcasted_iota(jnp.int32, (SNAPS, NY), 1)
    base = jnp.broadcast_to(base_ref[...], (SNAPS, NY))
    coef[0] = 0.1 - 0.3 * base
    coef[1] = 0.1 + 0.3 * base
    coef[2] = jnp.where(lane == NY - 1, 0.0, 0.1)
    coef[3] = jnp.where(lane == 0, 0.0, 0.1)
    coef[4] = 0.3 * jnp.broadcast_to(shear_ref[...], (SNAPS, NY))

    for c in range(2):
        snaps_in[c].wait()
        if c == 1:
            for i in range(LOADS):
                load(i).start()
        turned = jnp.swapaxes(snaps[:, c], 0, 1)
        own[pl.ds(2, NX), c] = turned
        code[:, c] = encode(turned)

    pl.semaphore_wait(barrier, ROWS - 1 + 5)

    fars = [
        send(
            code.at[pl.ds(at - 2, count)], code_d.at[pl.ds(at, count)],
            far_send.at[j], far_recv.at[j], row, far_col,
        )
        for j, (at, count) in enumerate(CUTS)
    ]
    at, count = CUTS[-1]
    both = send(
        code.at[pl.ds(at - 2, count)], code_p.at[pl.ds(at, count)],
        both_send.at[0], both_recv.at[0], row, far_side,
    )
    halos = [
        send(code.at[pl.ds(NX - 2, 2)], code_d.at[pl.ds(0, 2)],
             halo_send.at[0], halo_recv.at[0], up, far_col),
        send(code.at[pl.ds(0, 2)], code_d.at[pl.ds(NX + 2, 2)],
             halo_send.at[1], halo_recv.at[1], down, far_col),
    ]
    for copy in [fars[0], fars[1]] + halos + fars[2:] + [both]:
        copy.start()
    relays = [
        send(code_d.at[pl.ds(NX, 2)], halo_code.at[pl.ds(0, 2)],
             halo_send.at[2], halo_recv.at[2], up, far_col),
        send(code_d.at[pl.ds(2, 2)], halo_code.at[pl.ds(2, 2)],
             halo_send.at[3], halo_recv.at[3], down, far_col),
    ]
    passes = [
        send(
            code_d.at[pl.ds(at, count)], code_p.at[pl.ds(at, count)],
            pass_send.at[j], pass_recv.at[j], row, side,
        )
        for j, (at, count) in enumerate(CUTS[:-1] + ((0, 2), (NX + 2, 2)))
    ]

    def turn(i, _):
        load(i).wait()
        for c in range(2):
            block = jnp.swapaxes(adj_raw[i, :, c], 0, 1)
            for x in range(NX):
                adj[2 * x + c, pl.ds(pl.multiple_of(i * BLOCK, BLOCK), BLOCK)] = block[x]
        return 0

    def turn_group(g):
        lax.fori_loop(4 * g, 4 * g + 4, turn, 0)

        def turn_round(k, _):
            adj_t[k, :, pl.ds(128 * g, 128)] = adj[TURNED + k, pl.ds(128 * g, 128)].T
            return 0

        lax.fori_loop(0, 2 * NX - TURNED, turn_round, 0)

    def step(ref, x):
        flow = [ref[x, 0], ref[x, 1]]
        values = []
        for c in range(2):
            here = flow[c]
            value = 0.6 * here + (coef[0] * ref[x + 1, c] + coef[1] * ref[x - 1, c])
            value += coef[2] * pltpu.roll(here, NY - 1, 1) + coef[3] * pltpu.roll(here, 1, 1)
            if c == 0:
                value -= coef[4] * flow[1]
            values.append(value)
        return values

    def own_first(x):
        values = step(own, x + 1)
        for c in range(2):
            own_one[x, c] = values[c]

    def own_second(x):
        values = step(own_one, x + 1)
        for c in range(2):
            own_adv[x, c] = values[c]
            low_own[2 * x + c, pl.ds(0, SNAPS)] = own_one[x + 1, c].astype(LOW)
            low_own[2 * x + c, pl.ds(SNAPS, SNAPS)] = values[c].astype(LOW)

    def inner_first(i, _):
        for k in range(2):
            own_first(2 * i + k)
        return 0

    def inner_second(i, _):
        for k in range(4):
            own_second(2 + 4 * i + k)
        return 0

    lax.fori_loop(1, NX // 2, inner_first, 0)
    lax.fori_loop(0, 3, inner_second, 0)
    to_side = [
        send(low_own.at[pl.ds(at, count)], low_side.at[pl.ds(at, count)],
             side_send.at[j], side_recv.at[j], row, side)
        for j, (at, count) in enumerate(((4, 24), (0, 4), (28, 4)))
    ]
    to_side[0].start()

    turn_group(0)
    for k in range(2):
        fars[k].wait_recv()
        relays[k].start()
        passes[k].start()
    turn_group(1)
    for k in range(2):
        halos[k].wait_recv()
        passes[5 + k].start()
    turn_group(2)
    fars[2].wait_recv()
    passes[2].start()
    turn_group(3)

    def states(refs, codes, firsts, seconds):
        code_ref, wide, one, low = refs
        for k in codes:
            for c in range(2):
                wide[k, c] = decode(code_ref[k, c])
        for x in firsts:
            values = step(wide, x + 1)
            for c in range(2):
                one[x, c] = values[c]
        for x in seconds:
            values = step(one, x + 1)
            for c in range(2):
                low[2 * x + c, pl.ds(0, SNAPS)] = one[x + 1, c].astype(LOW)
                low[2 * x + c, pl.ds(SNAPS, SNAPS)] = values[c].astype(LOW)

    direct = (code_d, far_d, one_d, low_d)
    passed = (code_p, far_p, one_p, low_p)

    def multiply(at, count=4):
        left = jnp.concatenate(
            [
                jnp.concatenate([ref[at + i] for ref in (low_own, low_side, low_d, low_p)], axis=0)
                for i in range(count)
            ],
            axis=1,
        )
        if at < TURNED:
            right = jnp.concatenate([adj[at + i] for i in range(count)], axis=1)
            product = lax.dot_general(left, right, NT, preferred_element_type=F32)
        else:
            right = adj_t[pl.ds(at - TURNED, count)].reshape(count * NY, ADJS)
            product = jnp.dot(left, right, preferred_element_type=F32)
        if at == 4:
            total[...] = product
        else:
            total[...] += product

    states(direct, range(8), range(6), range(4))
    fars[3].wait_recv()
    passes[3].start()
    for copy in (passes[5], passes[1], passes[2]):
        copy.wait_recv()
    states(passed, range(8), range(6), range(4))
    fars[4].wait_recv()
    passes[4].start()

    relays[0].wait_recv()
    relays[1].wait_recv()
    for k in range(2):
        for c in range(2):
            own[k, c] = decode(halo_code[k, c])
            own[NX + 2 + k, c] = decode(halo_code[2 + k, c])
    for x in (0, 1, NX, NX + 1):
        own_first(x)
    for x in (0, 1, NX - 2, NX - 1):
        own_second(x)
    to_side[1].start()
    to_side[2].start()

    to_side[0].wait_recv()
    multiply(4)
    states(direct, range(8, 12), range(6, 10), range(4, 8))
    passes[3].wait_recv()
    states(passed, range(8, 12), range(6, 10), range(4, 8))

    for copy in (passes[0], passes[6]):
        copy.wait_recv()
    multiply(8)
    states(direct, (12, 13, 16, 17, 18, 19), (10, 11, 16, 17), (8, 9))
    passes[4].wait_recv()
    multiply(12)
    states(passed, (12, 13, 16, 17, 18, 19), (10, 11, 16, 17), (8, 9))
    to_side[1].wait_recv()
    multiply(0)

    fars[5].wait_recv()
    multiply(16)
    states(direct, (14, 15), range(12, 16), range(10, 16))
    both.wait_recv()
    to_side[2].wait_recv()
    states(passed, (14, 15), range(12, 16), range(10, 16))
    multiply(20)
    multiply(24, 8)

    for g in range(8):
        who = (col, side, far_col, far_side)[g // 2]
        for k in range(4):
            part[(4 * (g % 2) + who) * 4 + k] = total[pl.ds(16 * g, 16), pl.ds(128 * k, 128)]

    for to in others():
        send(part.at[to], gather.at[row], sum_sem.at[0], sum_sem.at[1], to, col).start()
    gather[row] = part[row]
    for c in range(2):
        adv_out[:, c] = jnp.swapaxes(own_adv[:, c], 0, 1)
    adv_copy = pltpu.make_async_copy(adv_out, adv_hbm, io_sem.at[1])
    adv_copy.start()
    rest = gather.at[pl.ds(0, ROWS - 1)]
    pltpu.make_async_copy(rest, rest, sum_sem.at[1]).wait()
    sums = [gather[t] for t in range(ROWS)]
    while len(sums) > 1:
        sums = [sums[t] + sums[t + 1] for t in range(0, len(sums), 2)]
    result[...] = sums[0]

    place = gram_hbm.at[
        row // 16,
        pl.ds(pl.multiple_of((row // 4) % 4 * 16, 16), 16),
        pl.ds(pl.multiple_of(row % 4 * 128, 128), 128),
    ]
    for to in others():
        send(result, place, sum_sem.at[2], sum_sem.at[3], to, col).start()
    own_piece = pltpu.make_async_copy(result, place, io_sem.at[0])
    own_piece.start()
    adv_copy.wait()
    for copy in halos + fars + relays + passes + to_side + [both]:
        copy.wait_send()
    own_piece.wait()
    pltpu.make_async_copy(rest, rest, sum_sem.at[0]).wait()
    pltpu.make_async_copy(rest, rest, sum_sem.at[2]).wait()
    pltpu.make_async_copy(rest, rest, sum_sem.at[3]).wait()


def hand_on(adv_in, gram_in, adv_hbm, gram_hbm, adv, gram, in_sem, out_sem):
    ways = [(adv_in.at[pl.ds(4 * i, 4)], adv.at[pl.ds(4 * i, 4)], adv_hbm.at[pl.ds(4 * i, 4)]) for i in range(4)]
    ways += [(gram_in.at[i], gram.at[i], gram_hbm.at[i]) for i in range(2)]
    for i, (src, mid, _) in enumerate(ways):
        pltpu.make_async_copy(src, mid, in_sem.at[i]).start()
    for i, (src, mid, dst) in enumerate(ways):
        pltpu.make_async_copy(src, mid, in_sem.at[i]).wait()
        pltpu.make_async_copy(mid, dst, out_sem.at[i]).start()
    for i, (_, mid, dst) in enumerate(ways):
        pltpu.make_async_copy(mid, dst, out_sem.at[i]).wait()


def per_device(snapshots, adjoint, base_flow, shear):
    vmem = pltpu.VMEM
    somewhere = pl.BlockSpec(memory_space=pl.ANY)
    shapes = (
        jax.ShapeDtypeStruct((SNAPS, 2, NX, NY), F32),
        jax.ShapeDtypeStruct((2, 64, ADJS), F32),
    )
    results = pl.pallas_call(
        kernel,
        out_shape=shapes,
        in_specs=[
            somewhere,
            somewhere,
            pl.BlockSpec(memory_space=vmem),
            pl.BlockSpec(memory_space=vmem),
        ],
        out_specs=(somewhere, somewhere),
        scratch_shapes=[
            vmem((SNAPS, 2, NX, NY), F32),
            vmem((5, SNAPS, NY), F32),
            vmem((NX + 4, 2, SNAPS, NY), F32),
            vmem((NX + 2, 2, SNAPS, NY), F32),
            vmem((NX, 2, SNAPS, NY), F32),
            vmem((SNAPS, 2, NX, NY), F32),
            vmem((NX, 2, SNAPS, NY), LOW),
            vmem((4, 2, SNAPS, NY), LOW),
            vmem((NX + 4, 2, SNAPS, NY), LOW),
            vmem((NX + 4, 2, SNAPS, NY), LOW),
            vmem((NX + 4, 2, SNAPS, NY), F32),
            vmem((NX + 4, 2, SNAPS, NY), F32),
            vmem((NX + 2, 2, SNAPS, NY), F32),
            vmem((NX + 2, 2, SNAPS, NY), F32),
            vmem((2 * NX, 2 * SNAPS, NY), LOW),
            vmem((2 * NX, 2 * SNAPS, NY), LOW),
            vmem((2 * NX, 2 * SNAPS, NY), LOW),
            vmem((2 * NX, 2 * SNAPS, NY), LOW),
            vmem((LOADS, BLOCK, 2, NX, NY), LOW),
            vmem((2 * NX, ADJS, NY), LOW),
            vmem((2 * NX - TURNED, NY, ADJS), LOW),
            vmem((128, ADJS), F32),
            vmem((ROWS, 16, 128), F32),
            vmem((ROWS, 16, 128), F32),
            vmem((16, 128), F32),
            pltpu.SemaphoreType.DMA((2,)),
            pltpu.SemaphoreType.DMA((LOADS,)),
            pltpu.SemaphoreType.DMA((4,)),
            pltpu.SemaphoreType.DMA((4,)),
            pltpu.SemaphoreType.DMA((6,)),
            pltpu.SemaphoreType.DMA((6,)),
            pltpu.SemaphoreType.DMA((7,)),
            pltpu.SemaphoreType.DMA((7,)),
            pltpu.SemaphoreType.DMA((3,)),
            pltpu.SemaphoreType.DMA((3,)),
            pltpu.SemaphoreType.DMA((1,)),
            pltpu.SemaphoreType.DMA((1,)),
            pltpu.SemaphoreType.DMA((4,)),
        ],
        compiler_params=pltpu.CompilerParams(
            collective_id=0, has_side_effects=True, vmem_limit_bytes=60 * 2**20
        ),
    )(snapshots, adjoint, base_flow.reshape(1, NY), shear.reshape(1, NY))
    return pl.pallas_call(
        hand_on,
        out_shape=shapes,
        in_specs=[somewhere, somewhere],
        out_specs=(somewhere, somewhere),
        scratch_shapes=[
            vmem((SNAPS, 2, NX, NY), F32),
            vmem((2, 64, ADJS), F32),
            pltpu.SemaphoreType.DMA((6,)),
            pltpu.SemaphoreType.DMA((6,)),
        ],
    )(*results)


def solution(mesh):
    in_specs = (P("cols", None, "rows", None), P("cols", None, "rows", None), P(), P())
    out_specs = (P("cols", None, "rows", None), P(None, None, "cols"))
    return jax.shard_map(
        per_device, mesh=mesh, in_specs=in_specs, out_specs=out_specs, check_vma=False
    )
```
